32 devices in a mesh: dp: 16 (over z, y, x), tensor: 2 (over core).
Axes of the slice: x: 2, y: 2, z: 4, core: 2. Of those that a mesh axis runs over, the one named last changes fastest.
Arguments:
- tokens: float32 [16384, 768], P(('dp', 'tensor')), may hold values from -6 to 6
- offsets: int32 [16, 16], P('dp'), may hold values from 0 to 1024, as said below
- w_qkv: bfloat16 [768, 3, 768], P('dp', None, 'tensor'), may hold values from -0.21875 to 0.21875
- w_attn_out: bfloat16 [768, 768], P('tensor', 'dp'), may hold values from -1.75 to 1.75
- w_in: bfloat16 [768, 2, 1152], P('dp', None, 'tensor'), may hold values from -0.21875 to 0.21875
- w_mlp_out: bfloat16 [1152, 768], P('tensor', 'dp'), may hold values from -0.1875 to 0.1875
- gain_attn: bfloat16 [768], P('dp'), may hold values from 0.099609375 to 1.8984375
- gain_mlp: bfloat16 [768], P('dp'), may hold values from 0.099609375 to 1.8984375
- cotangent: float32 [16384, 768], P(('dp', 'tensor')), may hold values from -6 to 6
Outputs:
- outputs: float32 [16384, 768], P(('dp', 'tensor'))
- grad_tokens: float32 [16384, 768], P(('dp', 'tensor'))
- grad_w_qkv: float32 [768, 3, 768], P('dp', None, 'tensor')
- grad_w_attn_out: float32 [768, 768], P('tensor', 'dp')
- grad_w_in: float32 [768, 2, 1152], P('dp', None, 'tensor')
- grad_w_mlp_out: float32 [1152, 768], P('tensor', 'dp')
- grad_gain_attn: float32 [768], P('dp')
- grad_gain_mlp: float32 [768], P('dp')
The draws below stay inside these ranges and needn't reach their ends.
Inputs may be any that keep to these rules, and one draw needn't show every extreme that they name: `offsets`: each row holds the first tokens of 16 sequences of one group of 1024 tokens, rising from 0 and never falling (equal entries are empty sequences); a sequence ends where the next begins, the last at 1024. No sequence has more than 512 tokens; in every row one has exactly 512 and holds the group's tokens 512 - 1 and 512.
All inputs are finite; a program needn't handle non-finite values.
Results may differ from the reference program's by a relative error of at most 0.018.
Values may be sent and summed in bfloat16 or wider, within the bound.
A program may use at most 128 MiB of HBM per device.

```python
import math
import jax
import jax.numpy as jnp
from jax import lax

D = 768
HEADS = 12
HEAD_DIM = 64
FF = 1152
SEQ_SLOTS = 16
GROUP = 1024
SEQ_MAX = 512
GROUPS = 16
TOKENS = 16384


def draw_offsets(key, part):
    key_start, key_left, key_right = jax.random.split(key, 3)
    left_count = (SEQ_SLOTS - 3) // 2
    right_count = SEQ_SLOTS - 3 - left_count
    long_start = jax.random.randint(key_start, (GROUPS, 1), 1, SEQ_MAX).astype(jnp.int32)
    left_cuts = jax.random.randint(key_left, (GROUPS, left_count), 0, 1 << 20).astype(jnp.int32) % (long_start + 1)
    right_raw = jax.random.randint(key_right, (GROUPS, right_count), 0, 1 << 20).astype(jnp.int32)
    right_cuts = long_start + SEQ_MAX + right_raw % (SEQ_MAX - long_start + 1)
    zeros_col = jnp.zeros((GROUPS, 1), jnp.int32)
    return jnp.concatenate([zeros_col, jnp.sort(left_cuts, axis=1), long_start, long_start + SEQ_MAX, jnp.sort(right_cuts, axis=1)], axis=1).astype(jnp.int32)


def raised(entries, own_key, source, target, shards_of, factor):
    owner, partner = [(jnp.arange(entries.shape[dim]) // (entries.shape[dim] // shards_of)).reshape([-1 if axis == dim else 1 for axis in range(entries.ndim)]) for dim in (source, target)]
    chosen = jax.random.permutation(own_key, shards_of)[partner]
    strong = (owner == chosen) | (owner == (partner + shards_of // 2) % shards_of)
    return jnp.where(strong, factor * entries, entries)


def block_levels(own_key, dims, shards, low, largest):
    def one(dim, parts):
        heights = jax.random.uniform(jax.random.fold_in(jax.random.fold_in(own_key, 6), dim), (parts,), jnp.float32, low / len(shards), largest / len(shards))
        return jnp.repeat(jnp.exp(heights), dims[dim] // parts).reshape((-1,) + (1,) * (len(dims) - dim - 1))

    level = one(*shards[0])
    for cut in shards[1:]:
        level = level * one(*cut)
    return level


def noise(rng, extent, scale, bound, pieces=(), kind=jnp.bfloat16):
    entries = scale * jax.random.normal(rng, extent, jnp.float32)
    if pieces:
        entries = entries * block_levels(rng, extent, pieces, -0.22, 0.18)
    return jnp.clip(entries, -bound, bound).astype(kind)


def bell_draw_with(rng, extent, deviation, limit, cuts, heavy, kind=jnp.bfloat16):
    result = deviation * jax.random.normal(rng, extent, jnp.float32)
    if cuts:
        result = result * block_levels(rng, extent, cuts, -0.22, 0.18)
    return jnp.clip(raised(result, jax.random.fold_in(rng, 3), *heavy), -limit, limit).astype(kind)


def setup_inputs(seed: int = 0) -> dict:
    keys = jax.random.split(jax.random.key(seed), 10)
    tokens = bell_draw_with(keys[0], (TOKENS, D), 1.0, 6.0, ((0, 32),), (0, 1, 32, 2.75), jnp.float32)
    offsets = draw_offsets(jax.random.fold_in(keys[9], 71), 0)
    w_qkv = noise(keys[2], (D, 3, D), D ** -0.5, 0.21875, ((0, 16), (2, 2)))
    w_attn_out = noise(keys[3], (D, D), (D // 64) ** -0.5, 1.75, ((0, 2), (1, 16)))
    w_in = noise(keys[4], (D, 2, FF), D ** -0.5, 0.21875, ((0, 16), (2, 2)))
    w_mlp_out = noise(keys[5], (FF, D), FF ** -0.5, 0.1875, ((0, 2), (1, 16)))
    gain_attn = jnp.clip(1.0 + 0.18 * jax.random.normal(keys[6], (D,), jnp.float32), 0.099609375, 1.8984375).astype(jnp.bfloat16)
    gain_mlp = jnp.clip(1.0 + 0.18 * jax.random.normal(keys[7], (D,), jnp.float32), 0.099609375, 1.8984375).astype(jnp.bfloat16)
    cotangent = bell_draw_with(keys[8], (TOKENS, D), 1.0, 6.0, ((0, 32),), (0, 1, 32, 2.75), jnp.float32)
    return dict(tokens=tokens, offsets=offsets, w_qkv=w_qkv, w_attn_out=w_attn_out, w_in=w_in, w_mlp_out=w_mlp_out, gain_attn=gain_attn, gain_mlp=gain_mlp, cotangent=cotangent)


EPSILON = 1e-05
ROPE_BASE = 160000.0
NEGATIVE = -1e+30

@jax.custom_vjp
def low(v):
    return lax.optimization_barrier(v.astype(jnp.bfloat16)).astype(jnp.float32)

@jax.custom_vjp
def low_back(v):
    return v

def low_keep(v):
    return (low(v), None)

def low_pass(kept, grad):
    return (grad,)

def back_keep(v):
    return (v, None)

def back_low(kept, grad):
    return (low(grad),)
low.defvjp(low_keep, low_pass)
low_back.defvjp(back_keep, back_low)

def seq_starts(offset_row, count_rows):
    position = jnp.arange(count_rows, dtype=jnp.int32)
    before = offset_row[None, :] <= position[:, None]
    return lax.optimization_barrier(jnp.max(jnp.where(before, offset_row[None, :], 0), axis=1)).astype(jnp.int32)

def rope_tables(starts):
    count_rows = starts.shape[0]
    position = jnp.arange(count_rows, dtype=jnp.int32) - starts
    half_dim = HEAD_DIM // 2
    inverse = jnp.power(jnp.float32(ROPE_BASE), -2.0 * jnp.arange(half_dim, dtype=jnp.float32) / HEAD_DIM)
    angles = position.astype(jnp.float32)[:, None] * inverse[None, :]
    return (jnp.cos(angles), jnp.sin(angles))

def rotate(head_rows, cosine_tab, sine_tab):
    half_dim = HEAD_DIM // 2
    first_half = head_rows[..., :half_dim]
    second = head_rows[..., half_dim:]
    cosine_b = cosine_tab[:, None, :]
    sine_b = sine_tab[:, None, :]
    return jnp.concatenate([first_half * cosine_b - second * sine_b, second * cosine_b + first_half * sine_b], axis=-1)

def layer_norm(inputs_v, gain_v):
    centre = inputs_v - lax.optimization_barrier(jnp.mean(inputs_v, axis=-1, keepdims=True))
    spread = lax.optimization_barrier(jnp.mean(centre * centre, axis=-1, keepdims=True))
    return centre * lax.rsqrt(spread + EPSILON) * gain_v

def group_forward(tokens_grp, offset_row, w_qkv, w_attn_out, w_in, w_mlp_out, gain_attn, gain_mlp):
    highest = lax.Precision.HIGHEST
    count_rows = tokens_grp.shape[0]
    scale_factor = 1.0 / math.sqrt(HEAD_DIM)
    starts = seq_starts(offset_row, count_rows)
    cosine_tab, sine_tab = rope_tables(starts)
    normed = low(layer_norm(tokens_grp, gain_attn))
    projected = low_back(jnp.einsum('td,dsk->tsk', normed, w_qkv, precision=highest))
    split_heads = projected.reshape(count_rows, 3, HEADS, HEAD_DIM)
    queries = low(rotate(split_heads[:, 0], cosine_tab, sine_tab))
    key_rows = low(rotate(split_heads[:, 1], cosine_tab, sine_tab))
    values = low(split_heads[:, 2])
    scores = low_back(jnp.einsum('qhe,khe->hqk', queries, key_rows, precision=highest) * scale_factor)
    same_seq = starts[:, None] == starts[None, :]
    weights_low = low(jax.nn.softmax(jnp.where(same_seq[None], scores, NEGATIVE), axis=-1))
    mixed_out = jnp.einsum('hqk,khe->qhe', weights_low, values, precision=highest)
    context = low_back(low(mixed_out.reshape(count_rows, HEADS * HEAD_DIM)))
    attended = low_back(jnp.dot(context, w_attn_out, precision=highest))
    hidden = tokens_grp + attended
    normed_mlp = low(layer_norm(hidden, gain_mlp))
    gate_up = low_back(jnp.einsum('td,dsf->tsf', normed_mlp, w_in, precision=highest))
    product = low(jax.nn.gelu(gate_up[:, 0], approximate=False) * gate_up[:, 1])
    branch = low_back(jnp.dot(product, w_mlp_out, precision=highest))
    return hidden + branch

def reference(tokens, offsets, w_qkv, w_attn_out, w_in, w_mlp_out, gain_attn, gain_mlp, cotangent):
    params = (w_qkv.astype(jnp.float32), w_attn_out.astype(jnp.float32), w_in.astype(jnp.float32), w_mlp_out.astype(jnp.float32), gain_attn.astype(jnp.float32), gain_mlp.astype(jnp.float32))
    grouped = tokens.reshape(GROUPS, GROUP, D)

    def forward(grouped_in, params_in):

        def one_group(group_pair):
            return group_forward(group_pair[0], group_pair[1], *params_in)
        return lax.map(jax.checkpoint(one_group), (grouped_in, offsets))
    outputs, pullback = jax.vjp(forward, grouped, params)
    grad_tokens, grad_params = pullback(cotangent.reshape(GROUPS, GROUP, D))
    return (outputs.reshape(TOKENS, D), grad_tokens.reshape(TOKENS, D), grad_params[0], grad_params[1], grad_params[2], grad_params[3], grad_params[4], grad_params[5])
```

```python
import math

import jax
import jax.numpy as jnp
from jax import lax
from jax.sharding import PartitionSpec as P

HEAD_DIM = 64


EPSILON = 1e-05
ROPE_BASE = 160000.0
NEGATIVE = -1e30


def seq_starts(offset_row, position):
    before = offset_row[None, :] <= position[:, None]
    return jnp.max(jnp.where(before, offset_row[None, :], 0), axis=1)


def rope_tables(position):
    half_dim = HEAD_DIM // 2
    inverse = jnp.power(
        jnp.float32(ROPE_BASE), -2.0 * jnp.arange(half_dim, dtype=jnp.float32) / HEAD_DIM
    )
    angles = position.astype(jnp.float32)[:, None] * inverse[None, :]
    return (jnp.cos(angles), jnp.sin(angles))


def rotate(head_rows, cosine_tab, sine_tab):
    half_dim = HEAD_DIM // 2
    first_half = head_rows[..., :half_dim]
    second = head_rows[..., half_dim:]
    cosine_b = cosine_tab[:, None, :]
    sine_b = sine_tab[:, None, :]
    return jnp.concatenate(
        [first_half * cosine_b - second * sine_b, second * cosine_b + first_half * sine_b], axis=-1
    )


def rotate_back(head_grads, cosine_tab, sine_tab):
    half_dim = HEAD_DIM // 2
    first_half = head_grads[..., :half_dim]
    second = head_grads[..., half_dim:]
    cosine_b = cosine_tab[:, None, :]
    sine_b = sine_tab[:, None, :]
    return jnp.concatenate(
        [first_half * cosine_b + second * sine_b, second * cosine_b - first_half * sine_b], axis=-1
    )


def layer_norm(inputs_v, gain_v):
    centre = inputs_v - jnp.mean(inputs_v, axis=-1, keepdims=True)
    spread = jnp.mean(centre * centre, axis=-1, keepdims=True)
    return centre * lax.rsqrt(spread + EPSILON) * gain_v


def levels_of(count):
    out = []
    stride = 1
    while stride < count:
        size = min(4, count // stride)
        out.append((stride, size))
        stride *= size
    return out


def swap_pairs(count, mask):
    return [(place, place ^ mask) for place in range(count)]


def gather_blocks(block):
    count = lax.axis_size("dp")
    me = lax.axis_index("dp")
    height, width = block.shape
    held = block.reshape(1, height, width)
    for stride, size in reversed(levels_of(count)):
        mine = (me // stride) % size
        taken = [held]
        for step in range(1, size):
            taken.append(lax.ppermute(held, "dp", swap_pairs(count, step * stride)))
        spread = jnp.zeros((held.shape[0], size, height, width), block.dtype)
        for step in range(size):
            spread = lax.dynamic_update_slice(
                spread, taken[step][:, None], (0, mine ^ step, 0, 0)
            )
        held = spread.reshape(held.shape[0] * size, height, width)
    return held.reshape(count * height, width)


def sum_blocks(terms):
    count = lax.axis_size("dp")
    me = lax.axis_index("dp")
    height = terms.shape[0] // count
    width = terms.shape[1]
    held = terms
    for stride, size in levels_of(count):
        mine = (me // stride) % size
        parts = held.reshape(-1, size, height, width)
        pick = lambda place: lax.dynamic_index_in_dim(parts, place, 1, keepdims=False)
        got = [
            lax.ppermute(pick(mine ^ step), "dp", swap_pairs(count, step * stride))
            for step in range(1, size)
        ]
        total = pick(mine).astype(jnp.float32)
        for other in got:
            total = total + other.astype(jnp.float32)
        held = total.astype(jnp.bfloat16)
    return total.reshape(height, width)


def other_half(local_rows):
    return lax.ppermute(local_rows, "tensor", [(0, 1), (1, 0)])


def spread_rows(local_rows):
    return jnp.concatenate([local_rows, other_half(local_rows)], axis=0)


def collect(partial_sums, rows_here):
    sent = other_half(partial_sums[rows_here:].astype(jnp.bfloat16))
    return partial_sums[:rows_here] + sent.astype(jnp.float32)


def two_terms(column):
    high = column.astype(jnp.bfloat16)
    rest = (column - lax.reduce_precision(column, 8, 7)).astype(jnp.bfloat16)
    return jnp.stack([high, rest], axis=1)


def padded(pieces):
    width = sum(piece.shape[1] for piece in pieces)
    short = -width % 128
    height = pieces[0].shape[0]
    if short:
        pieces = pieces + [jnp.zeros((height, short), jnp.bfloat16)]
    return jnp.concatenate(pieces, axis=1)


def block_scores(query_block, start_block, key_rows, starts, scale_factor):
    raw_scores = (
        jnp.einsum("qhe,khe->hqk", query_block, key_rows, preferred_element_type=jnp.float32)
        * scale_factor
    )
    same_seq = start_block[:, None] == starts[None, :]
    return jnp.where(same_seq[None], raw_scores, NEGATIVE)


def attention_forward(queries, key_rows, values, starts, scale_factor):
    group_rows, heads_here, head_dim = queries.shape
    block_rows = min(512, group_rows)
    block_count = group_rows // block_rows

    def one_block(block_in):
        query_block, start_block = block_in
        masked = block_scores(query_block, start_block, key_rows, starts, scale_factor)
        row_max = jnp.max(masked, axis=-1, keepdims=True)
        exp_terms = jnp.exp(masked - row_max)
        row_total = jnp.sum(exp_terms, axis=-1, keepdims=True)
        softmax_w = exp_terms / row_total
        mixed_out = jnp.einsum(
            "hqk,khe->qhe",
            softmax_w.astype(jnp.bfloat16),
            values,
            preferred_element_type=jnp.float32,
        )
        return (mixed_out, (row_max + jnp.log(row_total))[..., 0])

    mixed_all, lse_stack = lax.map(
        one_block,
        (
            queries.reshape(block_count, block_rows, heads_here, head_dim),
            starts.reshape(block_count, block_rows),
        ),
    )
    return (mixed_all.reshape(group_rows, heads_here, head_dim), lse_stack)


def attention_backward(queries, key_rows, values, starts, lse_stack, grad_out, scale_factor):
    group_rows, heads_here, head_dim = queries.shape
    block_rows = min(512, group_rows)
    block_count = group_rows // block_rows

    def one_block(carry_in, block_in):
        grad_keys, grad_values = carry_in
        query_block, start_block, lse_block, grad_block = block_in
        masked = block_scores(query_block, start_block, key_rows, starts, scale_factor)
        softmax_w = jnp.exp(masked - lse_block[..., None])
        grad_values = grad_values + jnp.einsum(
            "hqk,qhe->khe",
            softmax_w.astype(jnp.bfloat16),
            grad_block,
            preferred_element_type=jnp.float32,
        )
        grad_probs = jnp.einsum(
            "qhe,khe->hqk", grad_block, values, preferred_element_type=jnp.float32
        )
        grad_scores = softmax_w * (
            grad_probs - jnp.sum(softmax_w * grad_probs, axis=-1, keepdims=True)
        )
        rounded = grad_scores.astype(jnp.bfloat16)
        grad_query = (
            jnp.einsum("hqk,khe->qhe", rounded, key_rows, preferred_element_type=jnp.float32)
            * scale_factor
        )
        grad_keys = (
            grad_keys
            + jnp.einsum("hqk,qhe->khe", rounded, query_block, preferred_element_type=jnp.float32)
            * scale_factor
        )
        return ((grad_keys, grad_values), grad_query)

    zero_grads = jnp.zeros((group_rows, heads_here, head_dim), jnp.float32)
    block_inputs = (
        queries.reshape(block_count, block_rows, heads_here, head_dim),
        starts.reshape(block_count, block_rows),
        lse_stack,
        grad_out.reshape(block_count, block_rows, heads_here, head_dim),
    )
    (grad_keys, grad_values), grad_queries = lax.scan(
        one_block, (zero_grads, zero_grads), block_inputs
    )
    return (grad_queries.reshape(group_rows, heads_here, head_dim), grad_keys, grad_values)


def shards(tokens, offsets, w_qkv, w_attn_out, w_in, w_mlp_out, gain_attn, gain_mlp, cotangent):
    rows_here = tokens.shape[0]
    group_rows = rows_here * lax.axis_size("tensor")
    model_here = w_qkv.shape[0]
    width_here = w_qkv.shape[2]
    hidden_here = w_in.shape[2]
    heads_here = width_here // HEAD_DIM
    scale_factor = 1.0 / math.sqrt(HEAD_DIM)
    half_at = lax.axis_index("tensor") * rows_here
    position = (jnp.arange(group_rows, dtype=jnp.int32) + half_at) % group_rows
    starts = seq_starts(offsets[0], position)
    cosine_tab, sine_tab = rope_tables(position - starts)

    attn_pack = gather_blocks(
        padded([w_qkv.reshape(model_here, 3 * width_here), w_attn_out.T, gain_attn[:, None]])
    )
    mlp_pack = gather_blocks(
        padded([w_in.reshape(model_here, 2 * hidden_here), w_mlp_out.T, gain_mlp[:, None]])
    )
    qkv_full = attn_pack[:, : 3 * width_here]
    attn_out_full = attn_pack[:, 3 * width_here : 4 * width_here]
    gain_one = attn_pack[:, 4 * width_here].astype(jnp.float32)
    mlp_in_full = mlp_pack[:, : 2 * hidden_here]
    mlp_out_full = mlp_pack[:, 2 * hidden_here : 3 * hidden_here]
    gain_two = mlp_pack[:, 3 * hidden_here].astype(jnp.float32)

    grad_rows = spread_rows(cotangent.astype(jnp.bfloat16))
    normed_all = spread_rows(layer_norm(tokens, gain_one).astype(jnp.bfloat16))
    projected = jnp.dot(normed_all, qkv_full, preferred_element_type=jnp.float32)
    split_heads = projected.reshape(group_rows, 3, heads_here, HEAD_DIM)
    queries = rotate(split_heads[:, 0], cosine_tab, sine_tab).astype(jnp.bfloat16)
    key_rows = rotate(split_heads[:, 1], cosine_tab, sine_tab).astype(jnp.bfloat16)
    values = split_heads[:, 2].astype(jnp.bfloat16)
    mixed_all, lse_stack = attention_forward(queries, key_rows, values, starts, scale_factor)
    context = mixed_all.reshape(group_rows, width_here).astype(jnp.bfloat16)
    attended = collect(dot_nt(context, attn_out_full), rows_here)
    hidden = tokens + attended
    mlp_rows = spread_rows(layer_norm(hidden, gain_two).astype(jnp.bfloat16))
    gate_up = jnp.dot(mlp_rows, mlp_in_full, preferred_element_type=jnp.float32)
    gate_part = gate_up[:, :hidden_here]
    up_part = gate_up[:, hidden_here:]
    bell = 0.5 * (1.0 + lax.erf(gate_part * math.sqrt(0.5)))
    activated = gate_part * bell
    slope = bell + gate_part * jnp.exp(-0.5 * gate_part * gate_part) * (1.0 / math.sqrt(2 * math.pi))
    product_rows = (activated * up_part).astype(jnp.bfloat16)
    grad_product = jnp.dot(grad_rows, mlp_out_full, preferred_element_type=jnp.float32)
    grad_gate_up = jnp.concatenate(
        [
            (grad_product * up_part * slope).astype(jnp.bfloat16),
            (grad_product * activated).astype(jnp.bfloat16),
        ],
        axis=1,
    )
    branch = collect(dot_nt(product_rows, mlp_out_full), rows_here)
    outputs = hidden + branch
    grad_normed_two = collect(dot_nt(grad_gate_up, mlp_in_full), rows_here)
    unused_two, norm_pull_two = jax.vjp(layer_norm, hidden, gain_two)
    grad_hidden_norm, grad_gain_two = norm_pull_two(grad_normed_two)
    grad_hidden = cotangent + grad_hidden_norm
    mlp_terms = padded(
        [
            dot_tn(mlp_rows, grad_gate_up).astype(jnp.bfloat16),
            dot_tn(grad_rows, product_rows).astype(jnp.bfloat16),
            two_terms(grad_gain_two),
        ]
    )
    mlp_sums = sum_blocks(mlp_terms)

    grad_hidden_rows = spread_rows(grad_hidden.astype(jnp.bfloat16))
    grad_context = jnp.dot(
        grad_hidden_rows, attn_out_full, preferred_element_type=jnp.float32
    ).astype(jnp.bfloat16)
    grad_queries, grad_keys, grad_values = attention_backward(
        queries,
        key_rows,
        values,
        starts,
        lse_stack,
        grad_context.reshape(group_rows, heads_here, HEAD_DIM),
        scale_factor,
    )
    grad_projected = jnp.concatenate(
        [
            rotate_back(grad_queries, cosine_tab, sine_tab).reshape(group_rows, width_here),
            rotate_back(grad_keys, cosine_tab, sine_tab).reshape(group_rows, width_here),
            grad_values.reshape(group_rows, width_here),
        ],
        axis=1,
    ).astype(jnp.bfloat16)
    grad_normed_one = collect(dot_nt(grad_projected, qkv_full), rows_here)
    unused_one, norm_pull_one = jax.vjp(layer_norm, tokens, gain_one)
    grad_tokens_norm, grad_gain_one = norm_pull_one(grad_normed_one)
    grad_tokens = grad_hidden + grad_tokens_norm
    attn_terms = padded(
        [
            dot_tn(normed_all, grad_projected).astype(jnp.bfloat16),
            dot_tn(grad_hidden_rows, context).astype(jnp.bfloat16),
            two_terms(grad_gain_one),
        ]
    )
    attn_sums = sum_blocks(attn_terms)

    gain_one_cols = attn_sums[:, 4 * width_here : 4 * width_here + 2].sum(axis=1)
    gain_two_cols = mlp_sums[:, 3 * hidden_here : 3 * hidden_here + 2].sum(axis=1)
    gains = jnp.stack([gain_one_cols, gain_two_cols])
    gains = gains + other_half(gains)
    return (
        outputs,
        grad_tokens,
        attn_sums[:, : 3 * width_here].reshape(model_here, 3, width_here),
        attn_sums[:, 3 * width_here : 4 * width_here].T,
        mlp_sums[:, : 2 * hidden_here].reshape(model_here, 2, hidden_here),
        mlp_sums[:, 2 * hidden_here : 3 * hidden_here].T,
        gains[0],
        gains[1],
    )


def dot_nt(left, right):
    return lax.dot_general(
        left, right, (((1,), (1,)), ((), ())), preferred_element_type=jnp.float32
    )


def dot_tn(left, right):
    return lax.dot_general(
        left, right, (((0,), (0,)), ((), ())), preferred_element_type=jnp.float32
    )


def solution(mesh):
    in_specs = (
        P(("dp", "tensor"), None),
        P("dp", None),
        P("dp", None, "tensor"),
        P("tensor", "dp"),
        P("dp", None, "tensor"),
        P("tensor", "dp"),
        P("dp"),
        P("dp"),
        P(("dp", "tensor"), None),
    )
    out_specs = (
        P(("dp", "tensor"), None),
        P(("dp", "tensor"), None),
        P("dp", None, "tensor"),
        P("tensor", "dp"),
        P("dp", None, "tensor"),
        P("tensor", "dp"),
        P("dp"),
        P("dp"),
    )
    return jax.shard_map(shards, mesh=mesh, in_specs=in_specs, out_specs=out_specs, check_vma=False)
```

```python
import functools
import math

import jax
import jax.numpy as jnp
from jax import lax
from jax.experimental import pallas as pl
from jax.experimental.pallas import tpu as pltpu
from jax.sharding import PartitionSpec as P

HEAD_DIM = 64


EPSILON = 1e-05
ROPE_BASE = 160000.0
NEGATIVE = -1e30
LANES = 128
QUERY_BLOCK = 256
SCALE = 1.0 / math.sqrt(HEAD_DIM)
VMEM_LIMIT = 48 * 1024 * 1024


def seq_starts(offset_row, position):
    before = offset_row[None, :] <= position[:, None]
    return jnp.max(jnp.where(before, offset_row[None, :], 0), axis=1)


def rope_tables(position):
    half_dim = HEAD_DIM // 2
    inverse = jnp.power(
        jnp.float32(ROPE_BASE), -2.0 * jnp.arange(half_dim, dtype=jnp.float32) / HEAD_DIM
    )
    angles = position.astype(jnp.float32)[:, None] * inverse[None, :]
    copies = LANES // half_dim
    cosine = jnp.cos(angles)
    sine = jnp.sin(angles)
    return (
        jnp.concatenate([cosine] * copies, axis=1),
        jnp.concatenate([-sine, sine] * (copies // 2), axis=1),
    )


def layer_norm(inputs_v, gain_v):
    centre = inputs_v - jnp.mean(inputs_v, axis=-1, keepdims=True)
    spread = jnp.mean(centre * centre, axis=-1, keepdims=True)
    return centre * lax.rsqrt(spread + EPSILON) * gain_v


def levels_of(count):
    out = []
    stride = 1
    while stride < count:
        size = min(4, count // stride)
        out.append((stride, size))
        stride *= size
    return out


def swap_pairs(count, mask):
    return [(place, place ^ mask) for place in range(count)]


def gather_blocks(block):
    count = lax.axis_size("dp")
    me = lax.axis_index("dp")
    height, width = block.shape
    held = block.reshape(1, height, width)
    for stride, size in reversed(levels_of(count)):
        mine = (me // stride) % size
        taken = [held]
        for step in range(1, size):
            taken.append(lax.ppermute(held, "dp", swap_pairs(count, step * stride)))
        spread = jnp.zeros((held.shape[0], size, height, width), block.dtype)
        for step in range(size):
            spread = lax.dynamic_update_slice(
                spread, taken[step][:, None], (0, mine ^ step, 0, 0)
            )
        held = spread.reshape(held.shape[0] * size, height, width)
    return held.reshape(count * height, width)


def sum_blocks(terms):
    count = lax.axis_size("dp")
    me = lax.axis_index("dp")
    height = terms.shape[0] // count
    width = terms.shape[1]
    held = terms
    for stride, size in levels_of(count):
        mine = (me // stride) % size
        parts = held.reshape(-1, size, height, width)
        pick = lambda place: lax.dynamic_index_in_dim(parts, place, 1, keepdims=False)
        got = [
            lax.ppermute(pick(mine ^ step), "dp", swap_pairs(count, step * stride))
            for step in range(1, size)
        ]
        total = pick(mine).astype(jnp.float32)
        for other in got:
            total = total + other.astype(jnp.float32)
        held = total.astype(jnp.bfloat16)
    return total.reshape(height, width)


def other_half(local_rows):
    return lax.ppermute(local_rows, "tensor", [(0, 1), (1, 0)])


def spread_rows(local_rows):
    return jnp.concatenate([local_rows, other_half(local_rows)], axis=0)


def collect(partial_sums, rows_here):
    sent = other_half(partial_sums[rows_here:].astype(jnp.bfloat16))
    return partial_sums[:rows_here] + sent.astype(jnp.float32)


def two_terms(column):
    high = column.astype(jnp.bfloat16)
    rest = (column - lax.reduce_precision(column, 8, 7)).astype(jnp.bfloat16)
    return jnp.stack([high, rest], axis=1)


def padded(pieces):
    width = sum(piece.shape[1] for piece in pieces)
    short = -width % 128
    height = pieces[0].shape[0]
    if short:
        pieces = pieces + [jnp.zeros((height, short), jnp.bfloat16)]
    return jnp.concatenate(pieces, axis=1)


def dot_nt(left, right):
    return lax.dot_general(
        left, right, (((1,), (1,)), ((), ())), preferred_element_type=jnp.float32
    )


def dot_tn(left, right):
    return lax.dot_general(
        left, right, (((0,), (0,)), ((), ())), preferred_element_type=jnp.float32
    )


def turn(rows, cosine, sine_signed, lane):
    half_dim = HEAD_DIM // 2
    ahead = pltpu.roll(rows, rows.shape[1] - half_dim, axis=1)
    behind = pltpu.roll(rows, half_dim, axis=1)
    swapped = jnp.where(lane % HEAD_DIM < half_dim, ahead, behind)
    return rows * cosine + swapped * sine_signed


def forward_kernel(
    normed_ref, wq_ref, wk_ref, wv_ref, cos_ref, sin_ref, srow_ref, scol_ref,
    q_ref, k_ref, v_ref, ctx_ref, lse_ref, vt_ref,
):
    rows = normed_ref.shape[0]
    block = min(QUERY_BLOCK, rows)
    normed = normed_ref[...]
    cosine = cos_ref[...]
    sine = sin_ref[...]
    lane = lax.broadcasted_iota(jnp.int32, (rows, LANES), 1)
    dot = functools.partial(jnp.dot, preferred_element_type=jnp.float32)
    q_ref[...] = turn(dot(normed, wq_ref[...]), cosine, sine, lane).astype(jnp.bfloat16)
    k_ref[...] = turn(dot(normed, wk_ref[...]), cosine, sine, lane).astype(jnp.bfloat16)
    values = dot(normed, wv_ref[...])
    v_ref[...] = values.astype(jnp.bfloat16)
    vt_ref[...] = values.T.astype(jnp.bfloat16)

    @pl.loop(0, rows // block)
    def _(step):
        at = pl.ds(pl.multiple_of(step * block, block), block)
        same = scol_ref[...] == srow_ref[:, at]
        parts = []
        for head in range(LANES // HEAD_DIM):
            cols = slice(head * HEAD_DIM, (head + 1) * HEAD_DIM)
            scores = dot_nt(k_ref[:, cols], q_ref[at, cols]) * SCALE
            scores = jnp.where(same, scores, NEGATIVE)
            top = jnp.max(scores, axis=0, keepdims=True)
            terms = jnp.exp(scores - top)
            total = jnp.sum(terms, axis=0, keepdims=True)
            weights = (terms * (1.0 / total)).astype(jnp.bfloat16)
            parts.append(dot(vt_ref[cols, :], weights))
            lse_ref[0, head : head + 1, at] = top + jnp.log(total)
        ctx_ref[at, :] = jnp.concatenate(parts, axis=0).T.astype(jnp.bfloat16)


def backward_kernel(
    grad_ref, wo_ref, q_ref, k_ref, v_ref, cos_ref, sin_ref, srow_ref, scol_ref, lse_ref,
    dq_ref, dk_ref, dv_ref, g_ref, kt_ref, acc_q, acc_k, acc_v,
):
    rows = grad_ref.shape[0]
    block = min(QUERY_BLOCK, rows)
    dot = functools.partial(jnp.dot, preferred_element_type=jnp.float32)
    g_ref[...] = dot(grad_ref[...], wo_ref[...]).astype(jnp.bfloat16)
    kt_ref[...] = k_ref[...].astype(jnp.float32).T.astype(jnp.bfloat16)
    acc_k[...] = jnp.zeros_like(acc_k)
    acc_v[...] = jnp.zeros_like(acc_v)

    @pl.loop(0, rows // block)
    def _(step):
        at = pl.ds(pl.multiple_of(step * block, block), block)
        same = scol_ref[...] == srow_ref[:, at]
        parts = []
        for head in range(LANES // HEAD_DIM):
            cols = slice(head * HEAD_DIM, (head + 1) * HEAD_DIM)
            query = q_ref[at, cols]
            grad = g_ref[at, cols]
            scores = dot_nt(k_ref[:, cols], query) * SCALE
            probs = jnp.exp(jnp.where(same, scores - lse_ref[0, head : head + 1, at], NEGATIVE))
            acc_v[:, cols] += dot(probs.astype(jnp.bfloat16), grad)
            grad_probs = dot_nt(v_ref[:, cols], grad)
            weighted = probs * grad_probs
            drop = jnp.sum(weighted, axis=0, keepdims=True)
            grad_scores = (weighted - probs * drop).astype(jnp.bfloat16)
            acc_k[:, cols] += dot(grad_scores, query)
            parts.append(dot(kt_ref[cols, :], grad_scores))
        acc_q[at, :] = jnp.concatenate(parts, axis=0).T

    cosine = cos_ref[...] * SCALE
    sine = sin_ref[...] * -SCALE
    lane = lax.broadcasted_iota(jnp.int32, (rows, LANES), 1)
    dq_ref[...] = turn(acc_q[...], cosine, sine, lane).astype(jnp.bfloat16)
    dk_ref[...] = turn(acc_k[...], cosine, sine, lane).astype(jnp.bfloat16)
    dv_ref[...] = acc_v[...].astype(jnp.bfloat16)


def whole(shape):
    return pl.BlockSpec(shape, lambda pair: (0,) * len(shape))


def column_block(rows, first):
    return pl.BlockSpec((rows, LANES), lambda pair: (0, first + pair))


def attention_forward(normed_all, attn_pack, cosine, sine, starts, width_here):
    rows, width = normed_all.shape
    pairs = width_here // LANES
    heads_each = LANES // HEAD_DIM
    low = jax.ShapeDtypeStruct((rows, width_here), jnp.bfloat16)
    return pl.pallas_call(
        forward_kernel,
        grid=(pairs,),
        out_shape=(low, low, low, low, jax.ShapeDtypeStruct((pairs, heads_each, rows), jnp.float32)),
        in_specs=[
            whole((rows, width)),
            column_block(width, 0),
            column_block(width, pairs),
            column_block(width, 2 * pairs),
            whole((rows, LANES)),
            whole((rows, LANES)),
            whole((1, rows)),
            whole((rows, 1)),
        ],
        out_specs=[column_block(rows, 0)] * 4
        + [pl.BlockSpec((1, heads_each, rows), lambda pair: (pair, 0, 0))],
        scratch_shapes=[pltpu.VMEM((LANES, rows), jnp.bfloat16)],
        compiler_params=pltpu.CompilerParams(vmem_limit_bytes=VMEM_LIMIT),
        cost_estimate=pl.CostEstimate(
            flops=2 * rows * width * 3 * width_here + 4 * rows * rows * width_here,
            bytes_accessed=2 * (rows * width + 3 * width * width_here + 4 * rows * width_here),
            transcendentals=rows * rows * width_here // HEAD_DIM,
        ),
    )(normed_all, attn_pack, attn_pack, attn_pack, cosine, sine, starts[None, :], starts[:, None])


def attention_backward(grad_rows, attn_pack, queries, key_rows, values, cosine, sine, starts, lse):
    rows, width = grad_rows.shape
    width_here = queries.shape[1]
    pairs = width_here // LANES
    heads_each = LANES // HEAD_DIM
    low = jax.ShapeDtypeStruct((rows, width_here), jnp.bfloat16)
    return pl.pallas_call(
        backward_kernel,
        grid=(pairs,),
        out_shape=(low, low, low),
        in_specs=[
            whole((rows, width)),
            column_block(width, 3 * pairs),
            column_block(rows, 0),
            column_block(rows, 0),
            column_block(rows, 0),
            whole((rows, LANES)),
            whole((rows, LANES)),
            whole((1, rows)),
            whole((rows, 1)),
            pl.BlockSpec((1, heads_each, rows), lambda pair: (pair, 0, 0)),
        ],
        out_specs=[column_block(rows, 0)] * 3,
        scratch_shapes=[
            pltpu.VMEM((rows, LANES), jnp.bfloat16),
            pltpu.VMEM((LANES, rows), jnp.bfloat16),
            pltpu.VMEM((rows, LANES), jnp.float32),
            pltpu.VMEM((rows, LANES), jnp.float32),
            pltpu.VMEM((rows, LANES), jnp.float32),
        ],
        compiler_params=pltpu.CompilerParams(vmem_limit_bytes=VMEM_LIMIT),
        cost_estimate=pl.CostEstimate(
            flops=2 * rows * width * width_here + 10 * rows * rows * width_here,
            bytes_accessed=2 * (rows * width + width * width_here + 7 * rows * width_here),
            transcendentals=rows * rows * width_here // HEAD_DIM,
        ),
    )(
        grad_rows, attn_pack, queries, key_rows, values, cosine, sine,
        starts[None, :], starts[:, None], lse,
    )


def shards(tokens, offsets, w_qkv, w_attn_out, w_in, w_mlp_out, gain_attn, gain_mlp, cotangent):
    rows_here = tokens.shape[0]
    group_rows = rows_here * lax.axis_size("tensor")
    model_here = w_qkv.shape[0]
    width_here = w_qkv.shape[2]
    hidden_here = w_in.shape[2]
    half_at = lax.axis_index("tensor") * rows_here
    position = (jnp.arange(group_rows, dtype=jnp.int32) + half_at) % group_rows
    starts = seq_starts(offsets[0], position)
    cosine_tab, sine_tab = rope_tables(position - starts)

    attn_pack = gather_blocks(
        padded([w_qkv.reshape(model_here, 3 * width_here), w_attn_out.T, gain_attn[:, None]])
    )
    mlp_pack = gather_blocks(
        padded([w_in.reshape(model_here, 2 * hidden_here), w_mlp_out.T, gain_mlp[:, None]])
    )
    qkv_full = attn_pack[:, : 3 * width_here]
    attn_out_full = attn_pack[:, 3 * width_here : 4 * width_here]
    gain_one = attn_pack[:, 4 * width_here].astype(jnp.float32)
    mlp_in_full = mlp_pack[:, : 2 * hidden_here]
    mlp_out_full = mlp_pack[:, 2 * hidden_here : 3 * hidden_here]
    gain_two = mlp_pack[:, 3 * hidden_here].astype(jnp.float32)

    grad_rows = spread_rows(cotangent.astype(jnp.bfloat16))
    normed_all = spread_rows(layer_norm(tokens, gain_one).astype(jnp.bfloat16))
    queries, key_rows, values, context, lse = attention_forward(
        normed_all, attn_pack, cosine_tab, sine_tab, starts, width_here
    )
    attended = collect(dot_nt(context, attn_out_full), rows_here)
    hidden = tokens + attended
    mlp_rows = spread_rows(layer_norm(hidden, gain_two).astype(jnp.bfloat16))
    gate_up = jnp.dot(mlp_rows, mlp_in_full, preferred_element_type=jnp.float32)
    gate_part = gate_up[:, :hidden_here]
    up_part = gate_up[:, hidden_here:]
    bell = 0.5 * (1.0 + lax.erf(gate_part * math.sqrt(0.5)))
    activated = gate_part * bell
    slope = bell + gate_part * jnp.exp(-0.5 * gate_part * gate_part) * (1.0 / math.sqrt(2 * math.pi))
    product_rows = (activated * up_part).astype(jnp.bfloat16)
    grad_product = jnp.dot(grad_rows, mlp_out_full, preferred_element_type=jnp.float32)
    grad_gate_up = jnp.concatenate(
        [
            (grad_product * up_part * slope).astype(jnp.bfloat16),
            (grad_product * activated).astype(jnp.bfloat16),
        ],
        axis=1,
    )
    branch = collect(dot_nt(product_rows, mlp_out_full), rows_here)
    outputs = hidden + branch
    grad_normed_two = collect(dot_nt(grad_gate_up, mlp_in_full), rows_here)
    unused_two, norm_pull_two = jax.vjp(layer_norm, hidden, gain_two)
    grad_hidden_norm, grad_gain_two = norm_pull_two(grad_normed_two)
    grad_hidden = cotangent + grad_hidden_norm
    mlp_terms = padded(
        [
            dot_tn(mlp_rows, grad_gate_up).astype(jnp.bfloat16),
            dot_tn(grad_rows, product_rows).astype(jnp.bfloat16),
            two_terms(grad_gain_two),
        ]
    )
    mlp_sums = sum_blocks(mlp_terms)

    grad_hidden_rows = spread_rows(grad_hidden.astype(jnp.bfloat16))
    grad_projected = jnp.concatenate(
        attention_backward(
            grad_hidden_rows, attn_pack, queries, key_rows, values,
            cosine_tab, sine_tab, starts, lse,
        ),
        axis=1,
    )
    grad_normed_one = collect(dot_nt(grad_projected, qkv_full), rows_here)
    unused_one, norm_pull_one = jax.vjp(layer_norm, tokens, gain_one)
    grad_tokens_norm, grad_gain_one = norm_pull_one(grad_normed_one)
    grad_tokens = grad_hidden + grad_tokens_norm
    attn_terms = padded(
        [
            dot_tn(normed_all, grad_projected).astype(jnp.bfloat16),
            dot_tn(grad_hidden_rows, context).astype(jnp.bfloat16),
            two_terms(grad_gain_one),
        ]
    )
    attn_sums = sum_blocks(attn_terms)

    gain_one_cols = attn_sums[:, 4 * width_here : 4 * width_here + 2].sum(axis=1)
    gain_two_cols = mlp_sums[:, 3 * hidden_here : 3 * hidden_here + 2].sum(axis=1)
    gains = jnp.stack([gain_one_cols, gain_two_cols])
    gains = gains + other_half(gains)
    return (
        outputs,
        grad_tokens,
        attn_sums[:, : 3 * width_here].reshape(model_here, 3, width_here),
        attn_sums[:, 3 * width_here : 4 * width_here].T,
        mlp_sums[:, : 2 * hidden_here].reshape(model_here, 2, hidden_here),
        mlp_sums[:, 2 * hidden_here : 3 * hidden_here].T,
        gains[0],
        gains[1],
    )


def solution(mesh):
    in_specs = (
        P(("dp", "tensor"), None),
        P("dp", None),
        P("dp", None, "tensor"),
        P("tensor", "dp"),
        P("dp", None, "tensor"),
        P("tensor", "dp"),
        P("dp"),
        P("dp"),
        P(("dp", "tensor"), None),
    )
    out_specs = (
        P(("dp", "tensor"), None),
        P(("dp", "tensor"), None),
        P("dp", None, "tensor"),
        P("tensor", "dp"),
        P("dp", None, "tensor"),
        P("tensor", "dp"),
        P("dp"),
        P("dp"),
    )
    return jax.shard_map(shards, mesh=mesh, in_specs=in_specs, out_specs=out_specs, check_vma=False)
```

```python
import functools
import math

import jax
import jax.numpy as jnp
from jax import lax
from jax.experimental import pallas as pl
from jax.experimental.pallas import tpu as pltpu
from jax.sharding import PartitionSpec as P

HEAD_DIM = 64


EPSILON = 1e-05
ROPE_BASE = 160000.0
NEGATIVE = -1e30
LANES = 128
QUERY_BLOCK = 256
SCALE = 1.0 / math.sqrt(HEAD_DIM)
VMEM_LIMIT = 48 * 1024 * 1024


def seq_starts(offset_row, position):
    before = offset_row[None, :] <= position[:, None]
    return jnp.max(jnp.where(before, offset_row[None, :], 0), axis=1)


def rope_tables(position):
    half_dim = HEAD_DIM // 2
    inverse = jnp.power(
        jnp.float32(ROPE_BASE), -2.0 * jnp.arange(half_dim, dtype=jnp.float32) / HEAD_DIM
    )
    angles = position.astype(jnp.float32)[:, None] * inverse[None, :]
    copies = LANES // half_dim
    cosine = jnp.cos(angles)
    sine = jnp.sin(angles)
    return (
        jnp.concatenate([cosine] * copies, axis=1),
        jnp.concatenate([-sine, sine] * (copies // 2), axis=1),
    )


def levels_of(count):
    out = []
    stride = 1
    while stride < count:
        size = min(4, count // stride)
        out.append((stride, size))
        stride *= size
    return out


def swap_pairs(count, mask):
    return [(place, place ^ mask) for place in range(count)]


def gather_step(held, stride, size):
    count = lax.axis_size("dp")
    mine = (lax.axis_index("dp") // stride) % size
    outer, height, width = held.shape
    taken = [held]
    for step in range(1, size):
        taken.append(lax.ppermute(held, "dp", swap_pairs(count, step * stride)))

    def place():
        spread = jnp.zeros((outer, size, height, width), held.dtype)
        for step in range(size):
            spread = lax.dynamic_update_slice(
                spread, taken[step][:, None], (0, mine ^ step, 0, 0)
            )
        return spread.reshape(outer * size, height, width)

    return place()


def after(later, *earlier):
    return lax.optimization_barrier((later, *earlier))[0]


def gather_both(first, second):
    one, two = first[None], second[None]
    for stride, size in reversed(levels_of(lax.axis_size("dp"))):
        one = gather_step(one, stride, size)
        two = gather_step(after(two, one), stride, size)
    return one.reshape(-1, one.shape[2]), two.reshape(-1, two.shape[2])


def sum_blocks(terms, *earlier):
    count = lax.axis_size("dp")
    me = lax.axis_index("dp")
    height = terms.shape[0] // count
    width = terms.shape[1]
    held = terms
    for stride, size in levels_of(count):
        mine = (me // stride) % size
        parts = held.reshape(-1, size, height, width)
        pick = lambda place: lax.dynamic_index_in_dim(parts, place, 1, keepdims=False)
        got = [
            lax.ppermute(pick(mine ^ step), "dp", swap_pairs(count, step * stride))
            for step in range(1, size)
        ]
        if earlier:
            got = lax.optimization_barrier((got, *earlier))[0]
            earlier = ()
        total = pick(mine).astype(jnp.float32)
        for other in got:
            total = total + other.astype(jnp.float32)
        held = total.astype(jnp.bfloat16)
    return total.reshape(height, width)


def other_half(local_rows):
    return lax.ppermute(local_rows, "tensor", [(0, 1), (1, 0)])


def spread_rows(local_rows):
    return jnp.concatenate([local_rows, other_half(local_rows)], axis=0)


def collect_own(partial_sums, rows_here):
    sent = other_half(partial_sums[rows_here:].astype(jnp.bfloat16))
    return partial_sums[:rows_here] + sent.astype(jnp.float32)


def collect_all(partial_sums, rows_here):
    got = other_half(partial_sums.astype(jnp.bfloat16))
    swapped = jnp.concatenate([got[rows_here:], got[:rows_here]], axis=0)
    return partial_sums + swapped.astype(jnp.float32)


def norm_parts(inputs_v):
    centre = inputs_v - jnp.mean(inputs_v, axis=-1, keepdims=True)
    spread = jnp.mean(centre * centre, axis=-1, keepdims=True)
    scale_v = lax.rsqrt(spread + EPSILON)
    return centre * scale_v, scale_v


def norm_backward(incoming, gain_v, unit, scale_v):
    scaled = incoming * gain_v
    mean_one = jnp.mean(scaled, axis=-1, keepdims=True)
    mean_two = jnp.mean(scaled * unit, axis=-1, keepdims=True)
    return scale_v * (scaled - mean_one - unit * mean_two)


def two_terms(column):
    high = column.astype(jnp.bfloat16)
    rest = (column - lax.reduce_precision(column, 8, 7)).astype(jnp.bfloat16)
    return jnp.stack([high, rest], axis=1)


def padded(pieces):
    width = sum(piece.shape[1] for piece in pieces)
    short = -width % 128
    height = pieces[0].shape[0]
    if short:
        pieces = pieces + [jnp.zeros((height, short), jnp.bfloat16)]
    return jnp.concatenate(pieces, axis=1)


def dot_nn(left, right):
    return jnp.dot(left, right, preferred_element_type=jnp.float32)


def dot_nt(left, right):
    return lax.dot_general(
        left, right, (((1,), (1,)), ((), ())), preferred_element_type=jnp.float32
    )


def dot_tn(left, right):
    return lax.dot_general(
        left, right, (((0,), (0,)), ((), ())), preferred_element_type=jnp.float32
    )


def turn(rows, cosine, sine_signed, lane):
    half_dim = HEAD_DIM // 2
    ahead = pltpu.roll(rows, rows.shape[1] - half_dim, axis=1)
    behind = pltpu.roll(rows, half_dim, axis=1)
    swapped = jnp.where(lane % HEAD_DIM < half_dim, ahead, behind)
    return rows * cosine + swapped * sine_signed


def forward_kernel(
    normed_ref, wq_ref, wk_ref, wv_ref, cos_ref, sin_ref, srow_ref, scol_ref,
    q_ref, k_ref, v_ref, ctx_ref, lse_ref, vt_ref,
):
    rows = normed_ref.shape[0]
    block = min(QUERY_BLOCK, rows)
    normed = normed_ref[...]
    cosine = cos_ref[...]
    sine = sin_ref[...]
    lane = lax.broadcasted_iota(jnp.int32, (rows, LANES), 1)
    dot = functools.partial(jnp.dot, preferred_element_type=jnp.float32)
    q_ref[...] = turn(dot(normed, wq_ref[...]), cosine, sine, lane).astype(jnp.bfloat16)
    k_ref[...] = turn(dot(normed, wk_ref[...]), cosine, sine, lane).astype(jnp.bfloat16)
    values = dot(normed, wv_ref[...])
    v_ref[...] = values.astype(jnp.bfloat16)
    vt_ref[...] = values.T.astype(jnp.bfloat16)

    @pl.loop(0, rows // block)
    def _(step):
        at = pl.ds(pl.multiple_of(step * block, block), block)
        same = scol_ref[...] == srow_ref[:, at]
        parts = []
        for head in range(LANES // HEAD_DIM):
            cols = slice(head * HEAD_DIM, (head + 1) * HEAD_DIM)
            scores = dot_nt(k_ref[:, cols], q_ref[at, cols]) * SCALE
            scores = jnp.where(same, scores, NEGATIVE)
            top = jnp.max(scores, axis=0, keepdims=True)
            terms = jnp.exp(scores - top)
            total = jnp.sum(terms, axis=0, keepdims=True)
            weights = (terms * (1.0 / total)).astype(jnp.bfloat16)
            parts.append(dot(vt_ref[cols, :], weights))
            lse_ref[0, head : head + 1, at] = top + jnp.log(total)
        ctx_ref[at, :] = jnp.concatenate(parts, axis=0).T.astype(jnp.bfloat16)


def backward_kernel(
    grad_ref, wo_ref, q_ref, k_ref, v_ref, cos_ref, sin_ref, srow_ref, scol_ref, lse_ref,
    dq_ref, dk_ref, dv_ref, g_ref, kt_ref, acc_q, acc_k, acc_v,
):
    rows = grad_ref.shape[0]
    block = min(QUERY_BLOCK, rows)
    dot = functools.partial(jnp.dot, preferred_element_type=jnp.float32)
    g_ref[...] = dot(grad_ref[...], wo_ref[...]).astype(jnp.bfloat16)
    kt_ref[...] = k_ref[...].astype(jnp.float32).T.astype(jnp.bfloat16)
    acc_k[...] = jnp.zeros_like(acc_k)
    acc_v[...] = jnp.zeros_like(acc_v)

    @pl.loop(0, rows // block)
    def _(step):
        at = pl.ds(pl.multiple_of(step * block, block), block)
        same = scol_ref[...] == srow_ref[:, at]
        parts = []
        for head in range(LANES // HEAD_DIM):
            cols = slice(head * HEAD_DIM, (head + 1) * HEAD_DIM)
            query = q_ref[at, cols]
            grad = g_ref[at, cols]
            scores = dot_nt(k_ref[:, cols], query) * SCALE
            probs = jnp.exp(jnp.where(same, scores - lse_ref[0, head : head + 1, at], NEGATIVE))
            acc_v[:, cols] += dot(probs.astype(jnp.bfloat16), grad)
            grad_probs = dot_nt(v_ref[:, cols], grad)
            weighted = probs * grad_probs
            drop = jnp.sum(weighted, axis=0, keepdims=True)
            grad_scores = (weighted - probs * drop).astype(jnp.bfloat16)
            acc_k[:, cols] += dot(grad_scores, query)
            parts.append(dot(kt_ref[cols, :], grad_scores))
        acc_q[at, :] = jnp.concatenate(parts, axis=0).T

    cosine = cos_ref[...] * SCALE
    sine = sin_ref[...] * -SCALE
    lane = lax.broadcasted_iota(jnp.int32, (rows, LANES), 1)
    dq_ref[...] = turn(acc_q[...], cosine, sine, lane).astype(jnp.bfloat16)
    dk_ref[...] = turn(acc_k[...], cosine, sine, lane).astype(jnp.bfloat16)
    dv_ref[...] = acc_v[...].astype(jnp.bfloat16)


def whole(shape):
    return pl.BlockSpec(shape, lambda pair: (0,) * len(shape))


def column_block(rows, first):
    return pl.BlockSpec((rows, LANES), lambda pair: (0, first + pair))


def attention_forward(normed_all, attn_pack, cosine, sine, starts, width_here):
    rows, width = normed_all.shape
    pairs = width_here // LANES
    heads_each = LANES // HEAD_DIM
    low = jax.ShapeDtypeStruct((rows, width_here), jnp.bfloat16)
    return pl.pallas_call(
        forward_kernel,
        grid=(pairs,),
        out_shape=(low, low, low, low, jax.ShapeDtypeStruct((pairs, heads_each, rows), jnp.float32)),
        in_specs=[
            whole((rows, width)),
            column_block(width, 0),
            column_block(width, pairs),
            column_block(width, 2 * pairs),
            whole((rows, LANES)),
            whole((rows, LANES)),
            whole((1, rows)),
            whole((rows, 1)),
        ],
        out_specs=[column_block(rows, 0)] * 4
        + [pl.BlockSpec((1, heads_each, rows), lambda pair: (pair, 0, 0))],
        scratch_shapes=[pltpu.VMEM((LANES, rows), jnp.bfloat16)],
        compiler_params=pltpu.CompilerParams(vmem_limit_bytes=VMEM_LIMIT),
        cost_estimate=pl.CostEstimate(
            flops=2 * rows * width * 3 * width_here + 4 * rows * rows * width_here,
            bytes_accessed=2 * (rows * width + 3 * width * width_here + 4 * rows * width_here),
            transcendentals=rows * rows * width_here // HEAD_DIM,
        ),
    )(normed_all, attn_pack, attn_pack, attn_pack, cosine, sine, starts[None, :], starts[:, None])


def attention_backward(grad_rows, attn_pack, queries, key_rows, values, cosine, sine, starts, lse):
    rows, width = grad_rows.shape
    width_here = queries.shape[1]
    pairs = width_here // LANES
    heads_each = LANES // HEAD_DIM
    low = jax.ShapeDtypeStruct((rows, width_here), jnp.bfloat16)
    return pl.pallas_call(
        backward_kernel,
        grid=(pairs,),
        out_shape=(low, low, low),
        in_specs=[
            whole((rows, width)),
            column_block(width, 0),
            column_block(rows, 0),
            column_block(rows, 0),
            column_block(rows, 0),
            whole((rows, LANES)),
            whole((rows, LANES)),
            whole((1, rows)),
            whole((rows, 1)),
            pl.BlockSpec((1, heads_each, rows), lambda pair: (pair, 0, 0)),
        ],
        out_specs=[column_block(rows, 0)] * 3,
        scratch_shapes=[
            pltpu.VMEM((rows, LANES), jnp.bfloat16),
            pltpu.VMEM((LANES, rows), jnp.bfloat16),
            pltpu.VMEM((rows, LANES), jnp.float32),
            pltpu.VMEM((rows, LANES), jnp.float32),
            pltpu.VMEM((rows, LANES), jnp.float32),
        ],
        compiler_params=pltpu.CompilerParams(vmem_limit_bytes=VMEM_LIMIT),
        cost_estimate=pl.CostEstimate(
            flops=2 * rows * width * width_here + 10 * rows * rows * width_here,
            bytes_accessed=2 * (rows * width + width * width_here + 7 * rows * width_here),
            transcendentals=rows * rows * width_here // HEAD_DIM,
        ),
    )(
        grad_rows, attn_pack, queries, key_rows, values, cosine, sine,
        starts[None, :], starts[:, None], lse,
    )


def shards(tokens, offsets, w_qkv, w_attn_out, w_in, w_mlp_out, gain_attn, gain_mlp, cotangent):
    rows_here = tokens.shape[0]
    group_rows = rows_here * lax.axis_size("tensor")
    model_here = w_qkv.shape[0]
    width_here = w_qkv.shape[2]
    hidden_here = w_in.shape[2]
    half_at = lax.axis_index("tensor") * rows_here
    position = (jnp.arange(group_rows, dtype=jnp.int32) + half_at) % group_rows
    starts = seq_starts(offsets[0], position)
    cosine_tab, sine_tab = rope_tables(position - starts)

    attn_pack, rest_pack = gather_both(
        padded([w_qkv.reshape(model_here, 3 * width_here), gain_attn[:, None]]),
        padded(
            [w_attn_out.T, w_in.reshape(model_here, 2 * hidden_here), w_mlp_out.T, gain_mlp[:, None]]
        ),
    )
    gain_one = attn_pack[:, 3 * width_here].astype(jnp.float32)
    qkv_full = attn_pack[:, : 3 * width_here]

    token_rows = spread_rows(tokens)
    cotangent_rows = spread_rows(cotangent)
    grad_rows = cotangent_rows.astype(jnp.bfloat16)
    unit_one, scale_one = norm_parts(token_rows)
    normed_all = (unit_one * gain_one).astype(jnp.bfloat16)
    queries, key_rows, values, context, lse = attention_forward(
        normed_all, attn_pack, cosine_tab, sine_tab, starts, width_here
    )

    mlp_at = width_here
    mlp_end = width_here + 2 * hidden_here
    attn_out_full = rest_pack[:, :width_here]
    mlp_in_full = rest_pack[:, mlp_at:mlp_end]
    mlp_out_full = rest_pack[:, mlp_end : mlp_end + hidden_here]
    gain_two = rest_pack[:, mlp_end + hidden_here].astype(jnp.float32)
    attended = collect_all(dot_nt(context, attn_out_full), rows_here)
    hidden = token_rows + attended
    unit_two, scale_two = norm_parts(hidden)
    mlp_rows = (unit_two * gain_two).astype(jnp.bfloat16)
    gate_part = dot_nn(mlp_rows, mlp_in_full[:, :hidden_here])
    up_part = dot_nn(mlp_rows, mlp_in_full[:, hidden_here:])
    grad_product = dot_nn(grad_rows, mlp_out_full)
    bell = 0.5 * (1.0 + lax.erf(gate_part * math.sqrt(0.5)))
    activated = gate_part * bell
    slope = bell + gate_part * jnp.exp(-0.5 * gate_part * gate_part) * (1.0 / math.sqrt(2 * math.pi))
    product_rows = (activated * up_part).astype(jnp.bfloat16)
    grad_gate_up = jnp.concatenate(
        [
            (grad_product * up_part * slope).astype(jnp.bfloat16),
            (grad_product * activated).astype(jnp.bfloat16),
        ],
        axis=1,
    )
    grad_normed_two = collect_all(dot_nt(grad_gate_up, mlp_in_full), rows_here)
    grad_hidden = cotangent_rows + norm_backward(grad_normed_two, gain_two, unit_two, scale_two)
    grad_gain_two = jnp.sum((grad_normed_two * unit_two)[:rows_here], axis=0)
    grad_hidden_rows = grad_hidden.astype(jnp.bfloat16)
    grads_three = attention_backward(
        grad_hidden_rows, rest_pack, queries, key_rows, values,
        cosine_tab, sine_tab, starts, lse,
    )
    mlp_terms = padded(
        [
            dot_tn(mlp_rows, grad_gate_up).astype(jnp.bfloat16),
            dot_tn(grad_rows, product_rows).astype(jnp.bfloat16),
            two_terms(grad_gain_two),
        ]
    )
    mlp_sums = sum_blocks(mlp_terms, grads_three[0])
    branch = collect_own(dot_nt(product_rows, mlp_out_full), rows_here)
    outputs = hidden[:rows_here] + branch

    grad_projected = jnp.concatenate(grads_three, axis=1)
    grad_normed_one = collect_own(dot_nt(grad_projected, qkv_full), rows_here)
    grad_tokens = grad_hidden[:rows_here] + norm_backward(
        grad_normed_one, gain_one, unit_one[:rows_here], scale_one[:rows_here]
    )
    grad_gain_one = jnp.sum(grad_normed_one * unit_one[:rows_here], axis=0)
    attn_terms = padded(
        [
            dot_tn(normed_all, grad_projected).astype(jnp.bfloat16),
            dot_tn(grad_hidden_rows, context).astype(jnp.bfloat16),
            two_terms(grad_gain_one),
        ]
    )
    attn_sums = sum_blocks(attn_terms)

    gain_one_cols = attn_sums[:, 4 * width_here : 4 * width_here + 2].sum(axis=1)
    gain_two_cols = mlp_sums[:, 3 * hidden_here : 3 * hidden_here + 2].sum(axis=1)
    gains = jnp.stack([gain_one_cols, gain_two_cols])
    gains = gains + other_half(gains)
    return (
        outputs,
        grad_tokens,
        attn_sums[:, : 3 * width_here].reshape(model_here, 3, width_here),
        attn_sums[:, 3 * width_here : 4 * width_here].T,
        mlp_sums[:, : 2 * hidden_here].reshape(model_here, 2, hidden_here),
        mlp_sums[:, 2 * hidden_here : 3 * hidden_here].T,
        gains[0],
        gains[1],
    )


def solution(mesh):
    in_specs = (
        P(("dp", "tensor"), None),
        P("dp", None),
        P("dp", None, "tensor"),
        P("tensor", "dp"),
        P("dp", None, "tensor"),
        P("tensor", "dp"),
        P("dp"),
        P("dp"),
        P(("dp", "tensor"), None),
    )
    out_specs = (
        P(("dp", "tensor"), None),
        P(("dp", "tensor"), None),
        P("dp", None, "tensor"),
        P("tensor", "dp"),
        P("dp", None, "tensor"),
        P("tensor", "dp"),
        P("dp"),
        P("dp"),
    )
    return jax.shard_map(shards, mesh=mesh, in_specs=in_specs, out_specs=out_specs, check_vma=False)
```

```python
import functools
import math

import jax
import jax.numpy as jnp
from jax import lax
from jax.experimental import pallas as pl
from jax.experimental.pallas import tpu as pltpu
from jax.sharding import PartitionSpec as P

HEAD_DIM = 64


EPSILON = 1e-05
ROPE_BASE = 160000.0
NEGATIVE = -1e30
LANES = 128
QUERY_BLOCK = 256
SCALE = 1.0 / math.sqrt(HEAD_DIM)
VMEM_LIMIT = 48 * 1024 * 1024


def seq_starts(offset_row, position):
    before = offset_row[None, :] <= position[:, None]
    return jnp.max(jnp.where(before, offset_row[None, :], 0), axis=1)


def rope_tables(position):
    half_dim = HEAD_DIM // 2
    inverse = jnp.power(
        jnp.float32(ROPE_BASE), -2.0 * jnp.arange(half_dim, dtype=jnp.float32) / HEAD_DIM
    )
    angles = position.astype(jnp.float32)[:, None] * inverse[None, :]
    copies = LANES // half_dim
    cosine = jnp.cos(angles)
    sine = jnp.sin(angles)
    return (
        jnp.concatenate([cosine] * copies, axis=1),
        jnp.concatenate([-sine, sine] * (copies // 2), axis=1),
    )


def levels_of(count):
    out = []
    stride = 1
    while stride < count:
        size = min(4, count // stride)
        out.append((stride, size))
        stride *= size
    return out


def swap_pairs(count, mask):
    return [(place, place ^ mask) for place in range(count)]


def send_step(held, stride, size):
    count = lax.axis_size("dp")
    return [held] + [
        lax.ppermute(held, "dp", swap_pairs(count, step * stride)) for step in range(1, size)
    ]


def place_step(taken, stride, size):
    mine = (lax.axis_index("dp") // stride) % size
    outer, height, width = taken[0].shape
    spread = jnp.zeros((outer, size, height, width), taken[0].dtype)
    for step in range(size):
        spread = lax.dynamic_update_slice(spread, taken[step][:, None], (0, mine ^ step, 0, 0))
    return spread.reshape(outer * size, height, width)


def after(later, *earlier):
    return lax.optimization_barrier((later, *earlier))[0]


def gather_both(first, second):
    one, two = first[None], second[None]
    taken = None
    for level in reversed(levels_of(lax.axis_size("dp"))):
        if taken is not None:
            two = place_step(taken, *last)
        one = place_step(send_step(one, *level), *level)
        taken = send_step(after(two, one), *level)
        last = level
    return one.reshape(-1, one.shape[2]), (taken, last)


def gather_rest(pending, *earlier):
    taken, level = pending
    taken = lax.optimization_barrier((taken, *earlier))[0]
    full = place_step(taken, *level)
    return full.reshape(-1, full.shape[2])


def sum_blocks(terms, *earlier):
    count = lax.axis_size("dp")
    me = lax.axis_index("dp")
    height = terms.shape[0] // count
    width = terms.shape[1]
    held = terms
    for stride, size in levels_of(count):
        mine = (me // stride) % size
        parts = held.reshape(-1, size, height, width)
        pick = lambda place: lax.dynamic_index_in_dim(parts, place, 1, keepdims=False)
        got = [
            lax.ppermute(pick(mine ^ step), "dp", swap_pairs(count, step * stride))
            for step in range(1, size)
        ]
        if earlier:
            got = lax.optimization_barrier((got, *earlier))[0]
            earlier = ()
        total = pick(mine).astype(jnp.float32)
        for other in got:
            total = total + other.astype(jnp.float32)
        held = total.astype(jnp.bfloat16)
    return total.reshape(height, width)


def other_half(local_rows):
    return lax.ppermute(local_rows, "tensor", [(0, 1), (1, 0)])


def spread_rows(local_rows):
    return jnp.concatenate([local_rows, other_half(local_rows)], axis=0)


def collect_own(partial_sums, rows_here):
    sent = other_half(partial_sums[rows_here:].astype(jnp.bfloat16))
    return partial_sums[:rows_here] + sent.astype(jnp.float32)


def collect_all(partial_sums, rows_here):
    got = other_half(partial_sums.astype(jnp.bfloat16))
    swapped = jnp.concatenate([got[rows_here:], got[:rows_here]], axis=0)
    return partial_sums + swapped.astype(jnp.float32)


def norm_parts(inputs_v):
    centre = inputs_v - jnp.mean(inputs_v, axis=-1, keepdims=True)
    spread = jnp.mean(centre * centre, axis=-1, keepdims=True)
    scale_v = lax.rsqrt(spread + EPSILON)
    return centre * scale_v, scale_v


def norm_backward(incoming, gain_v, unit, scale_v):
    scaled = incoming * gain_v
    mean_one = jnp.mean(scaled, axis=-1, keepdims=True)
    mean_two = jnp.mean(scaled * unit, axis=-1, keepdims=True)
    return scale_v * (scaled - mean_one - unit * mean_two)


def two_terms(column):
    high = column.astype(jnp.bfloat16)
    rest = (column - lax.reduce_precision(column, 8, 7)).astype(jnp.bfloat16)
    return jnp.stack([high, rest], axis=1)


def padded(pieces):
    width = sum(piece.shape[1] for piece in pieces)
    short = -width % 128
    height = pieces[0].shape[0]
    if short:
        pieces = pieces + [jnp.zeros((height, short), jnp.bfloat16)]
    return jnp.concatenate(pieces, axis=1)


def dot_nn(left, right):
    return jnp.dot(left, right, preferred_element_type=jnp.float32)


def dot_nt(left, right):
    return lax.dot_general(
        left, right, (((1,), (1,)), ((), ())), preferred_element_type=jnp.float32
    )


def dot_tn(left, right):
    return lax.dot_general(
        left, right, (((0,), (0,)), ((), ())), preferred_element_type=jnp.float32
    )


def turn(rows, cosine, sine_signed, lane):
    half_dim = HEAD_DIM // 2
    ahead = pltpu.roll(rows, rows.shape[1] - half_dim, axis=1)
    behind = pltpu.roll(rows, half_dim, axis=1)
    swapped = jnp.where(lane % HEAD_DIM < half_dim, ahead, behind)
    return rows * cosine + swapped * sine_signed


def forward_kernel(
    normed_ref, wq_ref, wk_ref, wv_ref, cos_ref, sin_ref, srow_ref, scol_ref,
    q_ref, k_ref, v_ref, ctx_ref, lse_ref, vt_ref,
):
    rows = normed_ref.shape[0]
    block = min(QUERY_BLOCK, rows)
    normed = normed_ref[...]
    cosine = cos_ref[...]
    sine = sin_ref[...]
    lane = lax.broadcasted_iota(jnp.int32, (rows, LANES), 1)
    dot = functools.partial(jnp.dot, preferred_element_type=jnp.float32)
    q_ref[...] = turn(dot(normed, wq_ref[...]), cosine, sine, lane).astype(jnp.bfloat16)
    k_ref[...] = turn(dot(normed, wk_ref[...]), cosine, sine, lane).astype(jnp.bfloat16)
    values = dot(normed, wv_ref[...])
    v_ref[...] = values.astype(jnp.bfloat16)
    vt_ref[...] = values.T.astype(jnp.bfloat16)

    @pl.loop(0, rows // block)
    def _(step):
        at = pl.ds(pl.multiple_of(step * block, block), block)
        same = scol_ref[...] == srow_ref[:, at]
        parts = []
        for head in range(LANES // HEAD_DIM):
            cols = slice(head * HEAD_DIM, (head + 1) * HEAD_DIM)
            scores = dot_nt(k_ref[:, cols], q_ref[at, cols]) * SCALE
            scores = jnp.where(same, scores, NEGATIVE)
            top = jnp.max(scores, axis=0, keepdims=True)
            terms = jnp.exp(scores - top)
            total = jnp.sum(terms, axis=0, keepdims=True)
            weights = (terms * (1.0 / total)).astype(jnp.bfloat16)
            parts.append(dot(vt_ref[cols, :], weights))
            lse_ref[0, head : head + 1, at] = top + jnp.log(total)
        ctx_ref[at, :] = jnp.concatenate(parts, axis=0).T.astype(jnp.bfloat16)


def backward_kernel(
    grad_ref, wo_ref, q_ref, k_ref, v_ref, cos_ref, sin_ref, srow_ref, scol_ref, lse_ref,
    dq_ref, dk_ref, dv_ref, g_ref, kt_ref, acc_q, acc_k, acc_v,
):
    rows = grad_ref.shape[0]
    block = min(QUERY_BLOCK, rows)
    dot = functools.partial(jnp.dot, preferred_element_type=jnp.float32)
    g_ref[...] = dot(grad_ref[...], wo_ref[...]).astype(jnp.bfloat16)
    kt_ref[...] = k_ref[...].astype(jnp.float32).T.astype(jnp.bfloat16)
    acc_k[...] = jnp.zeros_like(acc_k)
    acc_v[...] = jnp.zeros_like(acc_v)

    @pl.loop(0, rows // block)
    def _(step):
        at = pl.ds(pl.multiple_of(step * block, block), block)
        same = scol_ref[...] == srow_ref[:, at]
        parts = []
        for head in range(LANES // HEAD_DIM):
            cols = slice(head * HEAD_DIM, (head + 1) * HEAD_DIM)
            query = q_ref[at, cols]
            grad = g_ref[at, cols]
            scores = dot_nt(k_ref[:, cols], query) * SCALE
            probs = jnp.exp(jnp.where(same, scores - lse_ref[0, head : head + 1, at], NEGATIVE))
            acc_v[:, cols] += dot(probs.astype(jnp.bfloat16), grad)
            grad_probs = dot_nt(v_ref[:, cols], grad)
            weighted = probs * grad_probs
            drop = jnp.sum(weighted, axis=0, keepdims=True)
            grad_scores = (weighted - probs * drop).astype(jnp.bfloat16)
            acc_k[:, cols] += dot(grad_scores, query)
            parts.append(dot(kt_ref[cols, :], grad_scores))
        acc_q[at, :] = jnp.concatenate(parts, axis=0).T

    cosine = cos_ref[...] * SCALE
    sine = sin_ref[...] * -SCALE
    lane = lax.broadcasted_iota(jnp.int32, (rows, LANES), 1)
    dq_ref[...] = turn(acc_q[...], cosine, sine, lane).astype(jnp.bfloat16)
    dk_ref[...] = turn(acc_k[...], cosine, sine, lane).astype(jnp.bfloat16)
    dv_ref[...] = acc_v[...].astype(jnp.bfloat16)


def whole(shape):
    return pl.BlockSpec(shape, lambda pair: (0,) * len(shape))


def column_block(rows, first):
    return pl.BlockSpec((rows, LANES), lambda pair: (0, first + pair))


def attention_forward(normed_all, attn_pack, cosine, sine, starts, width_here):
    rows, width = normed_all.shape
    pairs = width_here // LANES
    heads_each = LANES // HEAD_DIM
    low = jax.ShapeDtypeStruct((rows, width_here), jnp.bfloat16)
    return pl.pallas_call(
        forward_kernel,
        grid=(pairs,),
        out_shape=(low, low, low, low, jax.ShapeDtypeStruct((pairs, heads_each, rows), jnp.float32)),
        in_specs=[
            whole((rows, width)),
            column_block(width, 0),
            column_block(width, pairs),
            column_block(width, 2 * pairs),
            whole((rows, LANES)),
            whole((rows, LANES)),
            whole((1, rows)),
            whole((rows, 1)),
        ],
        out_specs=[column_block(rows, 0)] * 4
        + [pl.BlockSpec((1, heads_each, rows), lambda pair: (pair, 0, 0))],
        scratch_shapes=[pltpu.VMEM((LANES, rows), jnp.bfloat16)],
        compiler_params=pltpu.CompilerParams(vmem_limit_bytes=VMEM_LIMIT),
        cost_estimate=pl.CostEstimate(
            flops=2 * rows * width * 3 * width_here + 4 * rows * rows * width_here,
            bytes_accessed=2 * (rows * width + 3 * width * width_here + 4 * rows * width_here),
            transcendentals=rows * rows * width_here // HEAD_DIM,
        ),
    )(normed_all, attn_pack, attn_pack, attn_pack, cosine, sine, starts[None, :], starts[:, None])


def attention_backward(grad_rows, attn_pack, queries, key_rows, values, cosine, sine, starts, lse):
    rows, width = grad_rows.shape
    width_here = queries.shape[1]
    pairs = width_here // LANES
    heads_each = LANES // HEAD_DIM
    low = jax.ShapeDtypeStruct((rows, width_here), jnp.bfloat16)
    return pl.pallas_call(
        backward_kernel,
        grid=(pairs,),
        out_shape=(low, low, low),
        in_specs=[
            whole((rows, width)),
            column_block(width, 0),
            column_block(rows, 0),
            column_block(rows, 0),
            column_block(rows, 0),
            whole((rows, LANES)),
            whole((rows, LANES)),
            whole((1, rows)),
            whole((rows, 1)),
            pl.BlockSpec((1, heads_each, rows), lambda pair: (pair, 0, 0)),
        ],
        out_specs=[column_block(rows, 0)] * 3,
        scratch_shapes=[
            pltpu.VMEM((rows, LANES), jnp.bfloat16),
            pltpu.VMEM((LANES, rows), jnp.bfloat16),
            pltpu.VMEM((rows, LANES), jnp.float32),
            pltpu.VMEM((rows, LANES), jnp.float32),
            pltpu.VMEM((rows, LANES), jnp.float32),
        ],
        compiler_params=pltpu.CompilerParams(vmem_limit_bytes=VMEM_LIMIT),
        cost_estimate=pl.CostEstimate(
            flops=2 * rows * width * width_here + 10 * rows * rows * width_here,
            bytes_accessed=2 * (rows * width + width * width_here + 7 * rows * width_here),
            transcendentals=rows * rows * width_here // HEAD_DIM,
        ),
    )(
        grad_rows, attn_pack, queries, key_rows, values, cosine, sine,
        starts[None, :], starts[:, None], lse,
    )


def shards(tokens, offsets, w_qkv, w_attn_out, w_in, w_mlp_out, gain_attn, gain_mlp, cotangent):
    rows_here = tokens.shape[0]
    group_rows = rows_here * lax.axis_size("tensor")
    model_here = w_qkv.shape[0]
    width_here = w_qkv.shape[2]
    hidden_here = w_in.shape[2]
    half_at = lax.axis_index("tensor") * rows_here
    position = (jnp.arange(group_rows, dtype=jnp.int32) + half_at) % group_rows
    starts = seq_starts(offsets[0], position)
    cosine_tab, sine_tab = rope_tables(position - starts)

    attn_pack, pending = gather_both(
        padded([w_qkv.reshape(model_here, 3 * width_here), gain_attn[:, None]]),
        padded(
            [w_attn_out.T, w_in.reshape(model_here, 2 * hidden_here), w_mlp_out.T, gain_mlp[:, None]]
        ),
    )
    gain_one = attn_pack[:, 3 * width_here].astype(jnp.float32)
    qkv_full = attn_pack[:, : 3 * width_here]

    token_rows = spread_rows(tokens)
    cotangent_rows = spread_rows(cotangent)
    grad_rows = cotangent_rows.astype(jnp.bfloat16)
    unit_one, scale_one = norm_parts(token_rows)
    normed_all = (unit_one * gain_one).astype(jnp.bfloat16)
    queries, key_rows, values, context, lse = attention_forward(
        normed_all, attn_pack, cosine_tab, sine_tab, starts, width_here
    )

    rest_pack = gather_rest(pending, lse)
    mlp_at = width_here
    mlp_end = width_here + 2 * hidden_here
    attn_out_full = rest_pack[:, :width_here]
    mlp_in_full = rest_pack[:, mlp_at:mlp_end]
    mlp_out_full = rest_pack[:, mlp_end : mlp_end + hidden_here]
    gain_two = rest_pack[:, mlp_end + hidden_here].astype(jnp.float32)
    attended = collect_all(dot_nt(context, attn_out_full), rows_here)
    hidden = token_rows + attended
    unit_two, scale_two = norm_parts(hidden)
    mlp_rows = (unit_two * gain_two).astype(jnp.bfloat16)
    gate_part = dot_nn(mlp_rows, mlp_in_full[:, :hidden_here])
    up_part = dot_nn(mlp_rows, mlp_in_full[:, hidden_here:])
    grad_product = dot_nn(grad_rows, mlp_out_full)
    bell = 0.5 * (1.0 + lax.erf(gate_part * math.sqrt(0.5)))
    activated = gate_part * bell
    slope = bell + gate_part * jnp.exp(-0.5 * gate_part * gate_part) * (1.0 / math.sqrt(2 * math.pi))
    product_rows = (activated * up_part).astype(jnp.bfloat16)
    grad_gate_up = jnp.concatenate(
        [
            (grad_product * up_part * slope).astype(jnp.bfloat16),
            (grad_product * activated).astype(jnp.bfloat16),
        ],
        axis=1,
    )
    grad_normed_two = collect_all(dot_nt(grad_gate_up, mlp_in_full), rows_here)
    grad_hidden = cotangent_rows + norm_backward(grad_normed_two, gain_two, unit_two, scale_two)
    grad_gain_two = jnp.sum((grad_normed_two * unit_two)[:rows_here], axis=0)
    grad_hidden_rows = grad_hidden.astype(jnp.bfloat16)
    grads_three = attention_backward(
        grad_hidden_rows, rest_pack, queries, key_rows, values,
        cosine_tab, sine_tab, starts, lse,
    )
    mlp_terms = padded(
        [
            dot_tn(mlp_rows, grad_gate_up).astype(jnp.bfloat16),
            dot_tn(grad_rows, product_rows).astype(jnp.bfloat16),
            two_terms(grad_gain_two),
        ]
    )
    mlp_sums = sum_blocks(mlp_terms, grads_three[0])
    branch = collect_own(dot_nt(product_rows, mlp_out_full), rows_here)
    outputs = hidden[:rows_here] + branch

    grad_projected = jnp.concatenate(grads_three, axis=1)
    grad_normed_one = collect_own(dot_nt(grad_projected, qkv_full), rows_here)
    grad_tokens = grad_hidden[:rows_here] + norm_backward(
        grad_normed_one, gain_one, unit_one[:rows_here], scale_one[:rows_here]
    )
    grad_gain_one = jnp.sum(grad_normed_one * unit_one[:rows_here], axis=0)
    attn_terms = padded(
        [
            dot_tn(normed_all, grad_projected).astype(jnp.bfloat16),
            dot_tn(grad_hidden_rows, context).astype(jnp.bfloat16),
            two_terms(grad_gain_one),
        ]
    )
    attn_sums = sum_blocks(attn_terms)

    gain_one_cols = attn_sums[:, 4 * width_here : 4 * width_here + 2].sum(axis=1)
    gain_two_cols = mlp_sums[:, 3 * hidden_here : 3 * hidden_here + 2].sum(axis=1)
    gains = jnp.stack([gain_one_cols, gain_two_cols])
    gains = gains + other_half(gains)
    return (
        outputs,
        grad_tokens,
        attn_sums[:, : 3 * width_here].reshape(model_here, 3, width_here),
        attn_sums[:, 3 * width_here : 4 * width_here].T,
        mlp_sums[:, : 2 * hidden_here].reshape(model_here, 2, hidden_here),
        mlp_sums[:, 2 * hidden_here : 3 * hidden_here].T,
        gains[0],
        gains[1],
    )


def solution(mesh):
    in_specs = (
        P(("dp", "tensor"), None),
        P("dp", None),
        P("dp", None, "tensor"),
        P("tensor", "dp"),
        P("dp", None, "tensor"),
        P("tensor", "dp"),
        P("dp"),
        P("dp"),
        P(("dp", "tensor"), None),
    )
    out_specs = (
        P(("dp", "tensor"), None),
        P(("dp", "tensor"), None),
        P("dp", None, "tensor"),
        P("tensor", "dp"),
        P("dp", None, "tensor"),
        P("tensor", "dp"),
        P("dp"),
        P("dp"),
    )
    return jax.shard_map(shards, mesh=mesh, in_specs=in_specs, out_specs=out_specs, check_vma=False)
```
